32 devices in a mesh: genome: 16 (over z, y, x), heads: 2 (over core).
Axes of the slice: x: 2, y: 2, z: 4, core: 2. Of those that a mesh axis runs over, the one named last changes fastest.
Arguments:
- features_in: bfloat16 [1536, 16384], P('heads', 'genome'), may hold values from -6 to 6
- norm_scale: float32 [2, 1536], P(None, 'heads'), may hold values from 0.5 to 2
- norm_shift: float32 [2, 1536], P(None, 'heads'), may hold values from -3 to 3
- conv_weight: bfloat16 [2, 3, 1536, 1536], P(None, None, 'heads'), may hold values from -0.09375 to 0.09375
- head_weight: bfloat16 [1536, 4096], P('heads'), may hold values from -0.15625 to 0.15625
- assay_head_lists: int32 [16, 4], P('genome'), may hold values from 0 to 31, as said below
- assay_list_counts: int32 [16], P('genome'), may hold values from 1 to 4, as said below
- targets: bfloat16 [16384, 4, 128], P('genome'), may hold values from 0 to 3
Outputs:
- features: bfloat16 [1536, 16384], P('heads', 'genome')
- head_grad: float32 [4096, 1536], P('genome', 'heads')
The draws below stay inside these ranges and needn't reach their ends.
Inputs may be any that keep to these rules, and one draw needn't show every extreme that they name: Slots at or past assay_list_counts of a bin block hold ids that are unused. Some bin block uses all 4 slots. `assay_head_lists`: the ids within one row are distinct.
All inputs are finite; a program needn't handle non-finite values.
Results may differ from the reference program's by a relative error of at most 0.0085.
Values may be sent and summed in bfloat16 or wider, within the bound.
A program may use at most 128 MiB of HBM per device.

```python
import math
import jax
import jax.numpy as jnp
from jax import lax

C = 1536
BLOCK = 128
TYPES = 4096
LIST = 4
LAYERS = 2
BASE_DILATION = 4
BIN_DEV = 1024
BIN_BLOCKS = 16
BINS = 16384
HEAD_BLOCK_COUNT = 32


def draw_assay_list_counts(key, part):
    key = jax.random.fold_in(key, 11)
    first, second, third = jax.random.split(key, 3)
    left = jax.random.randint(first, (BIN_BLOCKS,), 1, LIST + 1)
    right = jax.random.randint(second, (BIN_BLOCKS,), 1, LIST + 1)
    counts = jnp.minimum(left, right)
    where = jax.random.randint(third, (), 0, BIN_BLOCKS)
    return counts.at[where].set(LIST).astype(jnp.int32)


def draw_assay_head_lists(key, part):
    key = jax.random.fold_in(key, 23)
    keys = jax.random.split(key, BIN_BLOCKS)
    perms = jax.vmap(lambda k: jax.random.permutation(k, HEAD_BLOCK_COUNT))(keys)
    return perms[:, :LIST].astype(jnp.int32)


def shard_levels(own_key, dims, cuts, low, high):
    gain = 1.0
    for dim, blocks in cuts:
        draws = jax.random.uniform(jax.random.fold_in(jax.random.fold_in(own_key, 6), dim), (blocks,), jnp.float32, low / len(cuts), high / len(cuts))
        gain = gain * jnp.repeat(jnp.exp(draws), dims[dim] // blocks).reshape((-1,) + (1,) * (len(dims) - 1 - dim))
    return gain


def noise(key, dims, width, reach, pieces=(), kind=jnp.bfloat16):
    entries = jax.random.normal(key, dims, jnp.float32) * width
    if len(pieces) > 0:
        entries = shard_levels(key, dims, pieces, -0.22, 0.18) * entries
    return jnp.clip(entries, min=-reach, max=reach).astype(kind)


def setup_inputs(seed: int = 0) -> dict:
    arg_keys = jax.random.split(jax.random.key(seed), 9)
    return {
        "features_in": noise(arg_keys[0], (C, BINS), 1.0, 6.0, ((0, 2), (1, 16))),
        "norm_scale": jnp.clip(jnp.exp(math.log(2.0) - 1.3862944 * jax.random.uniform(arg_keys[1], (LAYERS, C), jnp.float32) ** shard_levels(arg_keys[1], (LAYERS, C), ((1, 2),), -0.2, 0.2)), 0.5, 2.0),
        "norm_shift": noise(arg_keys[2], (LAYERS, C), 0.5, 3.0, ((1, 2),), jnp.float32),
        "conv_weight": noise(arg_keys[3], (LAYERS, 3, C, C), (3 * C) ** -0.5, 0.09375, ((2, 2),)),
        "head_weight": noise(arg_keys[4], (C, TYPES), C ** -0.5, 0.15625, ((0, 2),)),
        "assay_head_lists": draw_assay_head_lists(jax.random.fold_in(arg_keys[8], 71), 0),
        "assay_list_counts": draw_assay_list_counts(jax.random.fold_in(arg_keys[8], 71), 0),
        "targets": jnp.clip(3.0 * jax.random.uniform(arg_keys[7], (BINS, LIST, BLOCK), jnp.float32) ** shard_levels(arg_keys[7], (BINS, LIST, BLOCK), ((0, 16),), -0.2, 0.2), 0.0, 3.0).astype(jnp.bfloat16),
    }


def reference(features_in, norm_scale, norm_shift, conv_weight, head_weight, assay_head_lists, assay_list_counts, targets):
    x = features_in
    for layer_index in range(LAYERS):
        dilation_step = BASE_DILATION * 2 ** layer_index
        u = jax.nn.gelu(x.astype(jnp.float32) * norm_scale[layer_index][:, None] + norm_shift[layer_index][:, None], approximate=False).astype(jnp.bfloat16)
        padded_input = jnp.pad(u, ((0, 0), (dilation_step, dilation_step)))
        acc = jnp.zeros((C, BINS), jnp.float32)
        for k in range(3):
            acc = acc + jnp.dot(conv_weight[layer_index, k], padded_input[:, k * dilation_step:k * dilation_step + BINS], preferred_element_type=jnp.float32)
        x = (x.astype(jnp.float32) + acc).astype(jnp.bfloat16)
    blocks = head_weight.reshape(C, HEAD_BLOCK_COUNT, BLOCK)
    rows_all = jnp.transpose(x.reshape(C, BIN_BLOCKS, BIN_DEV), (1, 0, 2))
    goals = targets.reshape(BIN_BLOCKS, BIN_DEV, LIST, BLOCK)
    slot_ids = jnp.arange(LIST, dtype=jnp.int32)

    def step(grad, items):
        rows, ids, count, goal = items
        chosen = blocks[:, ids].astype(jnp.float32)
        rows_f = rows.astype(jnp.float32)
        z = jnp.einsum('ci,cst->ist', rows_f, chosen)
        active = (slot_ids < count).astype(jnp.float32)
        slope = ((jax.nn.softplus(z) - goal.astype(jnp.float32)) * jax.nn.sigmoid(z) * active[None, :, None] / BIN_DEV).astype(jnp.bfloat16)
        term = jnp.einsum('ist,ci->stc', slope.astype(jnp.float32), rows_f)
        return grad.at[ids].add(term), 0

    grad0 = jnp.zeros((HEAD_BLOCK_COUNT, BLOCK, C), jnp.float32)
    grad, ignored_value = lax.scan(step, grad0, (rows_all, assay_head_lists, assay_list_counts, goals))
    return x, grad.reshape(TYPES, C)
```

```python
import functools

import jax
import jax.numpy as jnp
from jax import lax
from jax.experimental import pallas as pl
from jax.experimental.pallas import tpu as pltpu
from jax.sharding import PartitionSpec as P

BLOCK = 128
TYPES = 4096
LIST = 4
LAYERS = 2
BASE_DILATION = 4
BIN_DEV = 1024
HEAD_BLOCK_COUNT = 32
HALO = 128
EDGE = 16
MESH = pl.DeviceIdType.MESH


def extended(cells, sides, width):
    for axis, dim in sides:
        count = lax.axis_size(axis)
        ends = count - 1
        head = lax.slice_in_dim(cells, 0, width, axis=dim)
        tail = lax.slice_in_dim(cells, cells.shape[dim] - width, cells.shape[dim], axis=dim)
        cells = jnp.concatenate(
            [
                lax.ppermute(tail, axis, [(i, (i + 1) % count) for i in range(ends)]),
                cells,
                lax.ppermute(head, axis, [((i + 1) % count, i) for i in range(ends)]),
            ],
            axis=dim,
        )
    return cells


def on_device_general(
    features_in,
    norm_scale,
    norm_shift,
    conv_weight,
    head_weight,
    assay_head_lists,
    assay_list_counts,
    targets,
):
    share_cols = features_in.shape[0]
    rows = features_in.shape[1]
    x = features_in
    for layer_index in range(LAYERS):
        dilation_step = BASE_DILATION * 2**layer_index
        taps = conv_weight[layer_index]
        u = jax.nn.gelu(
            x.astype(jnp.float32) * norm_scale[layer_index][:, None]
            + norm_shift[layer_index][:, None],
            approximate=False,
        ).astype(jnp.bfloat16)
        padded_input = extended(u, (("genome", 1),), dilation_step)
        piece = lax.all_gather(padded_input, "heads", axis=0, tiled=True)
        branch = jnp.zeros((share_cols, rows), jnp.float32)
        for k in range(3):
            branch = branch + jnp.dot(
                taps[k],
                piece[:, k * dilation_step : k * dilation_step + rows],
                preferred_element_type=jnp.float32,
            )
        x = (x.astype(jnp.float32) + branch).astype(jnp.bfloat16)
    ids = assay_head_lists[0]
    count = assay_list_counts[0]
    blocks = head_weight.reshape(share_cols, HEAD_BLOCK_COUNT, BLOCK)
    chosen = blocks[:, ids]
    active = (jnp.arange(LIST, dtype=jnp.int32) < count).astype(jnp.float32)
    partial_z = jnp.einsum("ci,cst->ist", x, chosen, preferred_element_type=jnp.float32)
    z = lax.psum(partial_z, "heads")
    slope = (
        (jax.nn.softplus(z) - targets.astype(jnp.float32))
        * jax.nn.sigmoid(z)
        * active[None, :, None]
        / BIN_DEV
    ).astype(jnp.bfloat16)
    term = jnp.einsum("ist,ci->stc", slope, x, preferred_element_type=jnp.float32)
    onehot = (ids[None, :] == jnp.arange(HEAD_BLOCK_COUNT, dtype=jnp.int32)[:, None]).astype(
        jnp.float32
    )
    dense = jnp.einsum("bs,stc->btc", onehot, term).reshape(TYPES, share_cols)
    head_grad = lax.psum_scatter(dense, "genome", scatter_dimension=0, tiled=True)
    return (x, head_grad)


def gelu(v):
    return 0.5 * v * (1.0 + lax.erf(v * 0.7071067811865476))


def pick_kernel(ids_ref, hw_ref, tg_ref, hw_out, tg_out):
    hw_out[...] = hw_ref[...].T
    tg_out[...] = tg_ref[...].T


def pick(ids, head_weight, goal):
    c = head_weight.shape[0]
    n = goal.shape[0]
    return pl.pallas_call(
        pick_kernel,
        grid_spec=pltpu.PrefetchScalarGridSpec(
            num_scalar_prefetch=1,
            grid=(LIST,),
            in_specs=[
                pl.BlockSpec((c, BLOCK), lambda s, ids: (0, ids[s])),
                pl.BlockSpec((n, BLOCK), lambda s, ids: (0, s)),
            ],
            out_specs=[
                pl.BlockSpec((BLOCK, c), lambda s, ids: (s, 0)),
                pl.BlockSpec((BLOCK, n), lambda s, ids: (s, 0)),
            ],
        ),
        out_shape=[
            jax.ShapeDtypeStruct((LIST * BLOCK, c), jnp.bfloat16),
            jax.ShapeDtypeStruct((LIST * BLOCK, n), jnp.bfloat16),
        ],
        name="pick",
    )(ids, head_weight, goal)


def trunk_kernel(
    feat, norm, act, hw, tg, w_hbm,
    x_out, term,
    w, xe, u, r, acc, edge_out, edge_in, z_own, z_out, z_in,
    w_sem, edge_send, edge_recv, u_send, u_recv, z_send, z_recv,
):
    c, n = feat.shape
    wide = n + HALO
    me = lax.axis_index("genome")
    h = lax.axis_index("heads")
    other = 1 - h
    count = lax.axis_size("genome")
    right, left = lax.rem(me + 1, count), lax.rem(me + count - 1, count)
    dot = functools.partial(jnp.dot, preferred_element_type=jnp.float32)

    loads = []
    for layer in range(LAYERS):
        for k in range(3):
            cp = pltpu.make_async_copy(w_hbm.at[layer, k], w.at[layer, k], w_sem.at[layer, k])
            cp.start()
            loads.append(cp)

    barrier = pltpu.get_barrier_semaphore()
    for dev in ((me, other), (left, h), (right, h)):
        pl.semaphore_signal(barrier, inc=1, device_id=dev, device_id_type=MESH)

    edge_out[0] = feat[:, 0:BLOCK].astype(jnp.float32).T[:EDGE].astype(jnp.bfloat16)
    edge_out[1] = (
        feat[:, n - BLOCK : n].astype(jnp.float32).T[BLOCK - EDGE :].astype(jnp.bfloat16)
    )
    pl.semaphore_wait(barrier, 3)
    edges = []
    for i, dev in enumerate((left, right)):
        cp = pltpu.make_async_remote_copy(
            edge_out.at[i], edge_in.at[i], edge_send.at[i], edge_recv.at[i],
            device_id=(dev, h), device_id_type=MESH,
        )
        cp.start()
        edges.append(cp)

    lane = lax.broadcasted_iota(jnp.int32, (1, wide), 1)
    inside = jnp.where(
        lane < n,
        1.0,
        jnp.where(
            lane < n + HALO // 2,
            jnp.where(me < count - 1, 1.0, 0.0),
            jnp.where(me > 0, 1.0, 0.0),
        ),
    ).astype(jnp.float32)

    pieces = 3
    step = c // pieces

    def u_copy(layer, m):
        rows = pl.ds(m * step, step)
        return pltpu.make_async_remote_copy(
            u.at[layer, 0, rows], u.at[layer, 1, rows],
            u_send.at[layer, m], u_recv.at[layer, m],
            device_id=(me, other), device_id_type=MESH,
        )

    def shifted(layer, half, rows, val):
        d = BASE_DILATION * 2**layer
        r[layer, half, 0, rows, :] = pltpu.roll(val, d, 1).astype(jnp.bfloat16)
        r[layer, half, 1, rows, :] = pltpu.roll(val, wide - d, 1).astype(jnp.bfloat16)

    def activate(layer, m):
        @pl.loop(0, step // BLOCK)
        def _(j):
            rows = pl.ds(pl.multiple_of(m * step + j * BLOCK, BLOCK), BLOCK)
            v = xe[layer, rows, :].astype(jnp.float32)
            a = norm[rows, layer : layer + 1]
            b = norm[rows, LAYERS + layer : LAYERS + layer + 1]
            val = (gelu(v * a + b) * inside).astype(jnp.bfloat16)
            u[layer, 0, rows, :] = val
            shifted(layer, 0, rows, val.astype(jnp.float32))

    xe[0, :, 0:n] = feat[...]
    for cp in edges:
        cp.wait()
    halo = jnp.concatenate(
        [
            edge_in[0].astype(jnp.float32),
            jnp.zeros((HALO - 2 * EDGE, c), jnp.float32),
            edge_in[1].astype(jnp.float32),
        ],
        axis=0,
    )
    xe[0, :, n:wide] = halo.T.astype(jnp.bfloat16)

    def own_part(layer, m, width):
        rows = pl.ds(pl.multiple_of(m * step, step), step)
        cols = pl.ds(pl.multiple_of(h * c, c), c)
        t = dot(w[layer, 0, rows, cols], r[layer, 0, 0, :, 0:width])
        t = t + dot(w[layer, 1, rows, cols], u[layer, 0, :, 0:width])
        t = t + dot(w[layer, 2, rows, cols], r[layer, 0, 1, :, 0:width])
        acc[rows, 0:width] = t

    def other_part(layer, m, width):
        rows = pl.ds(pl.multiple_of(m * step, step), step)
        cols = pl.ds(pl.multiple_of(other * c, c), c)
        t = acc[rows, 0:width] + dot(w[layer, 0, rows, cols], r[layer, 1, 0, :, 0:width])
        t = t + dot(w[layer, 1, rows, cols], u[layer, 1, :, 0:width])
        t = t + dot(w[layer, 2, rows, cols], r[layer, 1, 1, :, 0:width])
        return rows, (xe[layer, rows, 0:width].astype(jnp.float32) + t).astype(jnp.bfloat16)

    copies = []
    for m in range(pieces):
        activate(0, m)
        cp = u_copy(0, m)
        cp.start()
        copies.append(cp)

    for layer in range(LAYERS):
        last = layer == LAYERS - 1
        width = n if last else wide
        for k in range(3):
            loads[3 * layer + k].wait()

        @pl.loop(0, pieces)
        def _(m, layer=layer, width=width):
            own_part(layer, m, width)

        for m in range(pieces):
            copies[m].wait_recv()

            @pl.loop(0, step // BLOCK)
            def _(j, m=m, layer=layer):
                rows = pl.ds(pl.multiple_of(m * step + j * BLOCK, BLOCK), BLOCK)
                shifted(layer, 1, rows, u[layer, 1, rows, :].astype(jnp.float32))

        for m in range(pieces):
            copies[m].wait_send()
        copies = []
        if last:

            @pl.loop(0, pieces)
            def _(m, layer=layer, width=width):
                rows, val = other_part(layer, m, width)
                x_out[rows, :] = val
        else:
            for m in range(pieces):
                rows, val = other_part(layer, m, width)
                xe[layer + 1, rows, :] = val
                activate(layer + 1, m)
                cp = u_copy(layer + 1, m)
                cp.start()
                copies.append(cp)

    groups = 2
    size = LIST * BLOCK // groups
    sums = []
    for s in range(groups):
        rows = pl.ds(s * size, size)
        part = dot(hw[rows, :], x_out[...])
        z_own[rows, :] = part
        z_out[rows, :] = part.astype(jnp.bfloat16)
        cp = pltpu.make_async_remote_copy(
            z_out.at[rows], z_in.at[rows], z_send.at[s], z_recv.at[s],
            device_id=(me, other), device_id_type=MESH,
        )
        cp.start()
        sums.append(cp)
    for s in range(groups):
        rows = pl.ds(s * size, size)
        sums[s].wait()
        z = z_own[rows, :] + z_in[rows, :].astype(jnp.float32)
        e = jnp.exp(-jnp.abs(z))
        soft = jnp.maximum(z, 0.0) + jnp.log1p(e)
        sig = jnp.where(z >= 0.0, 1.0, e) / (1.0 + e)
        slope = (
            (soft - tg[rows, :].astype(jnp.float32)) * sig * (act[rows, :] / BIN_DEV)
        ).astype(jnp.bfloat16)
        term[rows, :] = lax.dot_general(
            slope, x_out[...], (((1,), (1,)), ((), ())), preferred_element_type=jnp.float32
        ).astype(jnp.bfloat16)


def trunk(feat, norm, act, hw, tg, w):
    c, n = feat.shape
    wide = n + HALO
    vmem = pl.BlockSpec(memory_space=pltpu.VMEM)
    bf16, f32 = jnp.bfloat16, jnp.float32
    return pl.pallas_call(
        trunk_kernel,
        out_shape=[
            jax.ShapeDtypeStruct((c, n), bf16),
            jax.ShapeDtypeStruct((LIST * BLOCK, c), bf16),
        ],
        in_specs=[vmem] * 5 + [pl.BlockSpec(memory_space=pl.ANY)],
        out_specs=[vmem, vmem],
        scratch_shapes=[
            pltpu.VMEM(w.shape, bf16),
            pltpu.VMEM((LAYERS, c, wide), bf16),
            pltpu.VMEM((LAYERS, 2, c, wide), bf16),
            pltpu.VMEM((LAYERS, 2, 2, c, wide), bf16),
            pltpu.VMEM((c, wide), f32),
            pltpu.VMEM((2, EDGE, c), bf16),
            pltpu.VMEM((2, EDGE, c), bf16),
            pltpu.VMEM((LIST * BLOCK, n), f32),
            pltpu.VMEM((LIST * BLOCK, n), bf16),
            pltpu.VMEM((LIST * BLOCK, n), bf16),
            pltpu.SemaphoreType.DMA((LAYERS, 3)),
            pltpu.SemaphoreType.DMA((2,)),
            pltpu.SemaphoreType.DMA((2,)),
            pltpu.SemaphoreType.DMA((LAYERS, 3)),
            pltpu.SemaphoreType.DMA((LAYERS, 3)),
            pltpu.SemaphoreType.DMA((2,)),
            pltpu.SemaphoreType.DMA((2,)),
        ],
        compiler_params=pltpu.CompilerParams(
            collective_id=0, has_side_effects=True, vmem_limit_bytes=60 * 2**20
        ),
        cost_estimate=pl.CostEstimate(
            flops=17 * 10**9, bytes_accessed=20 * 2**20, transcendentals=0
        ),
        name="trunk",
    )(feat, norm, act, hw, tg, w)


def scatter_kernel(
    chunks, table, term, out,
    mine, send2, keep, recv2, send3, recv3,
    s1, r1, s2, r2, s3, r3,
    *theirs,
):
    me = lax.axis_index("genome")
    h = lax.axis_index("heads")
    x, y, z = lax.rem(me, 2), lax.rem(me // 2, 2), me // 4
    depth = lax.axis_size("genome") // 4
    across_x = (z * 2 + y) * 2 + (1 - x)
    across_y = (z * 2 + (1 - y)) * 2 + x
    part = mine.shape[-1]

    barrier = pltpu.get_barrier_semaphore()
    peers = [lax.rem(z + i, depth) * 4 + y * 2 + x for i in range(1, depth)]
    for dev in [across_x, across_y] + peers:
        pl.semaphore_signal(barrier, inc=1, device_id=(dev, h), device_id_type=MESH)
    for p in range(chunks):
        for s in range(LIST):
            mine[p, s] = term[s * BLOCK : (s + 1) * BLOCK, p * part : (p + 1) * part]
        mine[p, LIST] = jnp.zeros((BLOCK, part), jnp.bfloat16)
        theirs[p][LIST] = jnp.zeros((BLOCK, part), jnp.bfloat16)
    pl.semaphore_wait(barrier, 2 + len(peers))

    first = []
    for p in range(chunks):
        cp = pltpu.make_async_remote_copy(
            mine.at[p, pl.ds(0, LIST)], theirs[p].at[pl.ds(0, LIST)], s1.at[p], r1.at[p],
            device_id=(across_x if p % 2 == 0 else across_y, h), device_id_type=MESH,
        )
        cp.start()
        first.append(cp)
    second = []
    for p in range(chunks):
        first[p].wait()
        o = p % 2

        @pl.loop(0, 2 * depth)
        def _(j, p=p, o=o):
            a = mine[p, table[o * 32 + j]].astype(jnp.float32)
            b = theirs[p][table[o * 32 + 16 + j]].astype(jnp.float32)
            send2[p, j] = (a + b).astype(jnp.bfloat16)

        cp = pltpu.make_async_remote_copy(
            send2.at[p], recv2.at[p], s2.at[p], r2.at[p],
            device_id=(across_y if p % 2 == 0 else across_x, h), device_id_type=MESH,
        )
        cp.start()
        second.append(cp)

        @pl.loop(0, 2 * depth)
        def _(j, p=p, o=o):
            a = mine[p, table[o * 32 + 8 + j]].astype(jnp.float32)
            b = theirs[p][table[o * 32 + 24 + j]].astype(jnp.float32)
            keep[p, j] = a + b

    third = []
    for p in range(chunks):
        second[p].wait()
        for i in range(1, depth):
            zz = lax.rem(z + i, depth)
            two = pl.ds(zz * 2, 2)
            send3[p, i - 1] = (
                keep[p, two] + recv2[p, two].astype(jnp.float32)
            ).astype(jnp.bfloat16)
            cp = pltpu.make_async_remote_copy(
                send3.at[p, i - 1], recv3.at[p, i - 1], s3.at[p, i - 1], r3.at[p, i - 1],
                device_id=(peers[i - 1], h), device_id_type=MESH,
            )
            cp.start()
            third.append(cp)
    for p in range(chunks):
        two = pl.ds(z * 2, 2)
        total = keep[p, two] + recv2[p, two].astype(jnp.float32)
        for i in range(1, depth):
            third[p * (depth - 1) + i - 1].wait()
            total = total + recv3[p, i - 1].astype(jnp.float32)
        for q in range(2):
            out[q * BLOCK : (q + 1) * BLOCK, p * part : (p + 1) * part] = total[q]


def scatter(table, term):
    c = term.shape[1]
    chunks = 6
    part = c // chunks
    bf16, f32 = jnp.bfloat16, jnp.float32
    vmem = pl.BlockSpec(memory_space=pltpu.VMEM)
    dma = pltpu.SemaphoreType.DMA
    return pl.pallas_call(
        functools.partial(scatter_kernel, chunks),
        out_shape=jax.ShapeDtypeStruct((2 * BLOCK, c), f32),
        in_specs=[pl.BlockSpec(memory_space=pltpu.SMEM), vmem],
        out_specs=vmem,
        scratch_shapes=[
            pltpu.VMEM((chunks, LIST + 1, BLOCK, part), bf16),
            pltpu.VMEM((chunks, 8, BLOCK, part), bf16),
            pltpu.VMEM((chunks, 8, BLOCK, part), f32),
            pltpu.VMEM((chunks, 8, BLOCK, part), bf16),
            pltpu.VMEM((chunks, 3, 2, BLOCK, part), bf16),
            pltpu.VMEM((chunks, 3, 2, BLOCK, part), bf16),
            dma((chunks,)), dma((chunks,)), dma((chunks,)), dma((chunks,)),
            dma((chunks, 3)), dma((chunks, 3)),
        ]
        + [pltpu.VMEM((LIST + 1, BLOCK, part), bf16)] * chunks,
        compiler_params=pltpu.CompilerParams(
            collective_id=1, has_side_effects=True, vmem_limit_bytes=48 * 2**20
        ),
        name="scatter",
    )(table, term)


def slot_table(ids):
    me = lax.axis_index("genome")
    x, y = me % 2, me // 2 % 2
    slot = jnp.arange(LIST, dtype=jnp.int32)
    j = jnp.arange(8, dtype=jnp.int32)

    def where_is(lists, blocks):
        hit = lists[None, :] == blocks[:, None]
        return jnp.min(jnp.where(hit, slot[None, :], LIST), axis=1)

    def across(bit):
        return lax.ppermute(ids, "genome", [(g, g ^ bit) for g in range(16)])

    def blocks(yy, xx):
        return j // 2 * 8 + yy * 4 + xx * 2 + j % 2

    ways = []
    for bit, on in ((1, blocks(1 - y, x)), (2, blocks(y, 1 - x))):
        wanted = jnp.concatenate([on, blocks(y, x)])
        ways += [where_is(ids, wanted), where_is(across(bit), wanted)]
    return jnp.concatenate(ways)


def on_device(
    features_in,
    norm_scale,
    norm_shift,
    conv_weight,
    head_weight,
    assay_head_lists,
    assay_list_counts,
    targets,
):
    ids = assay_head_lists[0]
    table = slot_table(ids)
    norm = jnp.concatenate([norm_scale, norm_shift], axis=0).T
    active = jnp.arange(LIST, dtype=jnp.int32) < assay_list_counts[0]
    act = jnp.repeat(active.astype(jnp.float32), BLOCK)[:, None]
    hw, tg = pick(ids, head_weight, targets.reshape(targets.shape[0], LIST * BLOCK))
    x, term = trunk(features_in, norm, act, hw, tg, conv_weight)
    return (x, scatter(table, term))


def solution(mesh):
    fits = mesh.shape["genome"] == 16 and mesh.shape["heads"] == 2
    return jax.shard_map(
        on_device if fits else on_device_general,
        mesh=mesh,
        in_specs=(
            P("heads", "genome"),
            P(None, "heads"),
            P(None, "heads"),
            P(None, None, "heads", None),
            P("heads", None),
            P("genome", None),
            P("genome"),
            P("genome", None, None),
        ),
        out_specs=(P("heads", "genome"), P("genome", "heads")),
        check_vma=False,
    )
```

```python
import functools

import jax
import jax.numpy as jnp
from jax import lax
from jax.experimental import pallas as pl
from jax.experimental.pallas import tpu as pltpu
from jax.sharding import PartitionSpec as P

BLOCK = 128
TYPES = 4096
LIST = 4
LAYERS = 2
BASE_DILATION = 4
BIN_DEV = 1024
HEAD_BLOCK_COUNT = 32
HALO = 128
EDGE = 16
MESH = pl.DeviceIdType.MESH


def extended(cells, sides, width):
    for axis, dim in sides:
        count = lax.axis_size(axis)
        ends = count - 1
        head = lax.slice_in_dim(cells, 0, width, axis=dim)
        tail = lax.slice_in_dim(cells, cells.shape[dim] - width, cells.shape[dim], axis=dim)
        cells = jnp.concatenate(
            [
                lax.ppermute(tail, axis, [(i, (i + 1) % count) for i in range(ends)]),
                cells,
                lax.ppermute(head, axis, [((i + 1) % count, i) for i in range(ends)]),
            ],
            axis=dim,
        )
    return cells


def on_device_general(
    features_in,
    norm_scale,
    norm_shift,
    conv_weight,
    head_weight,
    assay_head_lists,
    assay_list_counts,
    targets,
):
    share_cols = features_in.shape[0]
    rows = features_in.shape[1]
    x = features_in
    for layer_index in range(LAYERS):
        dilation_step = BASE_DILATION * 2**layer_index
        taps = conv_weight[layer_index]
        u = jax.nn.gelu(
            x.astype(jnp.float32) * norm_scale[layer_index][:, None]
            + norm_shift[layer_index][:, None],
            approximate=False,
        ).astype(jnp.bfloat16)
        padded_input = extended(u, (("genome", 1),), dilation_step)
        piece = lax.all_gather(padded_input, "heads", axis=0, tiled=True)
        branch = jnp.zeros((share_cols, rows), jnp.float32)
        for k in range(3):
            branch = branch + jnp.dot(
                taps[k],
                piece[:, k * dilation_step : k * dilation_step + rows],
                preferred_element_type=jnp.float32,
            )
        x = (x.astype(jnp.float32) + branch).astype(jnp.bfloat16)
    ids = assay_head_lists[0]
    count = assay_list_counts[0]
    blocks = head_weight.reshape(share_cols, HEAD_BLOCK_COUNT, BLOCK)
    chosen = blocks[:, ids]
    active = (jnp.arange(LIST, dtype=jnp.int32) < count).astype(jnp.float32)
    partial_z = jnp.einsum("ci,cst->ist", x, chosen, preferred_element_type=jnp.float32)
    z = lax.psum(partial_z, "heads")
    slope = (
        (jax.nn.softplus(z) - targets.astype(jnp.float32))
        * jax.nn.sigmoid(z)
        * active[None, :, None]
        / BIN_DEV
    ).astype(jnp.bfloat16)
    term = jnp.einsum("ist,ci->stc", slope, x, preferred_element_type=jnp.float32)
    onehot = (ids[None, :] == jnp.arange(HEAD_BLOCK_COUNT, dtype=jnp.int32)[:, None]).astype(
        jnp.float32
    )
    dense = jnp.einsum("bs,stc->btc", onehot, term).reshape(TYPES, share_cols)
    head_grad = lax.psum_scatter(dense, "genome", scatter_dimension=0, tiled=True)
    return (x, head_grad)


def gelu(v):
    return 0.5 * v * (1.0 + lax.erf(v * 0.7071067811865476))


def pick_kernel(ids_ref, hw_ref, hw_out):
    hw_out[...] = hw_ref[...].T


def pick(ids, head_weight):
    c = head_weight.shape[0]
    return pl.pallas_call(
        pick_kernel,
        grid_spec=pltpu.PrefetchScalarGridSpec(
            num_scalar_prefetch=1,
            grid=(LIST,),
            in_specs=[pl.BlockSpec((c, BLOCK), lambda s, ids: (0, ids[s]))],
            out_specs=pl.BlockSpec((BLOCK, c), lambda s, ids: (s, 0)),
        ),
        out_shape=jax.ShapeDtypeStruct((LIST * BLOCK, c), jnp.bfloat16),
        name="pick",
    )(ids, head_weight)


def trunk_kernel(
    feat, norm, act, ids, hw, goal, w_hbm,
    x_out, term, lists,
    w, xe, u, r, acc, edge_out, edge_in, z_own, z_out, z_in,
    tg, w_sem, edge_send, edge_recv, u_send, u_recv, z_send, z_recv, id_send, id_recv,
):
    c, n = feat.shape
    wide = n + HALO
    me = lax.axis_index("genome")
    h = lax.axis_index("heads")
    other = 1 - h
    count = lax.axis_size("genome")
    right, left = lax.rem(me + 1, count), lax.rem(me + count - 1, count)
    dot = functools.partial(jnp.dot, preferred_element_type=jnp.float32)

    loads = []
    for layer in range(LAYERS):
        for k in range(3):
            cp = pltpu.make_async_copy(w_hbm.at[layer, k], w.at[layer, k], w_sem.at[layer, k])
            cp.start()
            loads.append(cp)

    barrier = pltpu.get_barrier_semaphore()
    near = [(flip(me, bit), h) for bit in NEAR]
    for dev in [(me, other), (left, h), (right, h)] + near:
        pl.semaphore_signal(barrier, inc=1, device_id=dev, device_id_type=MESH)

    edge_out[0] = feat[:, 0:BLOCK].astype(jnp.float32).T[:EDGE].astype(jnp.bfloat16)
    edge_out[1] = (
        feat[:, n - BLOCK : n].astype(jnp.float32).T[BLOCK - EDGE :].astype(jnp.bfloat16)
    )
    for s in range(LIST):
        tg[s * BLOCK : (s + 1) * BLOCK, :] = goal[:, s * BLOCK : (s + 1) * BLOCK].T
    pl.semaphore_wait(barrier, 3 + len(near))
    edges = []
    for i, dev in enumerate((left, right)):
        cp = pltpu.make_async_remote_copy(
            edge_out.at[i], edge_in.at[i], edge_send.at[i], edge_recv.at[i],
            device_id=(dev, h), device_id_type=MESH,
        )
        cp.start()
        edges.append(cp)
    asked = []
    for i, dev in enumerate(near):
        cp = pltpu.make_async_remote_copy(
            ids, lists.at[i], id_send.at[i], id_recv.at[i],
            device_id=dev, device_id_type=MESH,
        )
        cp.start()
        asked.append(cp)

    lane = lax.broadcasted_iota(jnp.int32, (1, wide), 1)
    inside = jnp.where(
        lane < n,
        1.0,
        jnp.where(
            lane < n + HALO // 2,
            jnp.where(me < count - 1, 1.0, 0.0),
            jnp.where(me > 0, 1.0, 0.0),
        ),
    ).astype(jnp.float32)

    pieces = 3
    step = c // pieces

    def u_copy(layer, m):
        rows = pl.ds(m * step, step)
        return pltpu.make_async_remote_copy(
            u.at[layer, 0, rows], u.at[layer, 1, rows],
            u_send.at[layer, m], u_recv.at[layer, m],
            device_id=(me, other), device_id_type=MESH,
        )

    def shifted(layer, half, rows, val):
        d = BASE_DILATION * 2**layer
        r[layer, half, 0, rows, :] = pltpu.roll(val, d, 1).astype(jnp.bfloat16)
        r[layer, half, 1, rows, :] = pltpu.roll(val, wide - d, 1).astype(jnp.bfloat16)

    def active(layer, rows, v, mask):
        a = norm[rows, layer : layer + 1]
        b = norm[rows, LAYERS + layer : LAYERS + layer + 1]
        val = gelu(v.astype(jnp.float32) * a + b)
        return (val if mask is None else val * mask).astype(jnp.bfloat16)

    def activate(layer, m):
        @pl.loop(0, step // BLOCK)
        def _(j):
            rows = pl.ds(pl.multiple_of(m * step + j * BLOCK, BLOCK), BLOCK)
            val = active(layer, rows, xe[layer, rows, :], inside)
            u[layer, 0, rows, :] = val

    def shift_own(layer):
        @pl.loop(0, c // BLOCK)
        def _(j):
            rows = pl.ds(pl.multiple_of(j * BLOCK, BLOCK), BLOCK)
            shifted(layer, 0, rows, u[layer, 0, rows, :].astype(jnp.float32))

    @pl.loop(0, c // BLOCK)
    def _(j):
        rows = pl.ds(pl.multiple_of(j * BLOCK, BLOCK), BLOCK)
        val = feat[rows, :]
        xe[0, rows, 0:n] = val
        u[0, 0, rows, 0:n] = active(0, rows, val, None)

    for cp in edges:
        cp.wait()
    halo = jnp.concatenate(
        [
            edge_in[0].astype(jnp.float32),
            jnp.zeros((HALO - 2 * EDGE, c), jnp.float32),
            edge_in[1].astype(jnp.float32),
        ],
        axis=0,
    )
    halo = halo.T
    xe[0, :, n:wide] = halo.astype(jnp.bfloat16)
    u[0, 0, :, n:wide] = active(0, slice(None), halo, inside[:, n:wide])

    def own_part(layer, m, width):
        rows = pl.ds(pl.multiple_of(m * step, step), step)
        cols = pl.ds(pl.multiple_of(h * c, c), c)
        t = dot(w[layer, 0, rows, cols], r[layer, 0, 0, :, 0:width])
        t = t + dot(w[layer, 1, rows, cols], u[layer, 0, :, 0:width])
        t = t + dot(w[layer, 2, rows, cols], r[layer, 0, 1, :, 0:width])
        acc[rows, 0:width] = t

    def other_part(layer, m, width):
        rows = pl.ds(pl.multiple_of(m * step, step), step)
        cols = pl.ds(pl.multiple_of(other * c, c), c)
        t = acc[rows, 0:width] + dot(w[layer, 0, rows, cols], r[layer, 1, 0, :, 0:width])
        t = t + dot(w[layer, 1, rows, cols], u[layer, 1, :, 0:width])
        t = t + dot(w[layer, 2, rows, cols], r[layer, 1, 1, :, 0:width])
        return rows, (xe[layer, rows, 0:width].astype(jnp.float32) + t).astype(jnp.bfloat16)

    copies = []
    for m in range(pieces):
        cp = u_copy(0, m)
        cp.start()
        copies.append(cp)

    for layer in range(LAYERS):
        last = layer == LAYERS - 1
        width = n if last else wide
        shift_own(layer)
        for k in range(3):
            loads[3 * layer + k].wait()

        @pl.loop(0, pieces)
        def _(m, layer=layer, width=width):
            own_part(layer, m, width)

        for m in range(pieces):
            copies[m].wait_recv()

            @pl.loop(0, step // BLOCK)
            def _(j, m=m, layer=layer):
                rows = pl.ds(pl.multiple_of(m * step + j * BLOCK, BLOCK), BLOCK)
                shifted(layer, 1, rows, u[layer, 1, rows, :].astype(jnp.float32))

        for m in range(pieces):
            copies[m].wait_send()
        copies = []
        if last:

            @pl.loop(0, pieces)
            def _(m, layer=layer, width=width):
                rows, val = other_part(layer, m, width)
                x_out[rows, :] = val
        else:
            for m in range(pieces):
                rows, val = other_part(layer, m, width)
                xe[layer + 1, rows, :] = val
                activate(layer + 1, m)
                cp = u_copy(layer + 1, m)
                cp.start()
                copies.append(cp)

    groups = 2
    size = LIST * BLOCK // groups
    sums = []
    for s in range(groups):
        rows = pl.ds(s * size, size)
        part = dot(hw[rows, :], x_out[...])
        z_own[rows, :] = part
        z_out[rows, :] = part.astype(jnp.bfloat16)
        cp = pltpu.make_async_remote_copy(
            z_out.at[rows], z_in.at[rows], z_send.at[s], z_recv.at[s],
            device_id=(me, other), device_id_type=MESH,
        )
        cp.start()
        sums.append(cp)
    for s in range(groups):
        rows = pl.ds(s * size, size)
        sums[s].wait()
        z = z_own[rows, :] + z_in[rows, :].astype(jnp.float32)
        e = jnp.exp(-jnp.abs(z))
        soft = jnp.maximum(z, 0.0) + jnp.log1p(e)
        sig = jnp.where(z >= 0.0, 1.0, e) / (1.0 + e)
        slope = (
            (soft - tg[rows, :].astype(jnp.float32)) * sig * (act[rows, :] / BIN_DEV)
        ).astype(jnp.bfloat16)
        term[rows, :] = lax.dot_general(
            slope, x_out[...], (((1,), (1,)), ((), ())), preferred_element_type=jnp.float32
        ).astype(jnp.bfloat16)
    for cp in asked:
        cp.wait()


def trunk(feat, norm, act, ids, hw, goal, w):
    c, n = feat.shape
    wide = n + HALO
    vmem = pl.BlockSpec(memory_space=pltpu.VMEM)
    bf16, f32 = jnp.bfloat16, jnp.float32
    return pl.pallas_call(
        trunk_kernel,
        out_shape=[
            jax.ShapeDtypeStruct((c, n), bf16),
            jax.ShapeDtypeStruct((LIST * BLOCK, c), bf16),
            jax.ShapeDtypeStruct((len(NEAR),) + ids.shape, jnp.int32),
        ],
        in_specs=[vmem] * 6 + [pl.BlockSpec(memory_space=pl.ANY)],
        out_specs=[vmem, vmem, vmem],
        scratch_shapes=[
            pltpu.VMEM(w.shape, bf16),
            pltpu.VMEM((LAYERS, c, wide), bf16),
            pltpu.VMEM((LAYERS, 2, c, wide), bf16),
            pltpu.VMEM((LAYERS, 2, 2, c, wide), bf16),
            pltpu.VMEM((c, wide), f32),
            pltpu.VMEM((2, EDGE, c), bf16),
            pltpu.VMEM((2, EDGE, c), bf16),
            pltpu.VMEM((LIST * BLOCK, n), f32),
            pltpu.VMEM((LIST * BLOCK, n), bf16),
            pltpu.VMEM((LIST * BLOCK, n), bf16),
            pltpu.VMEM((LIST * BLOCK, n), bf16),
            pltpu.SemaphoreType.DMA((LAYERS, 3)),
            pltpu.SemaphoreType.DMA((2,)),
            pltpu.SemaphoreType.DMA((2,)),
            pltpu.SemaphoreType.DMA((LAYERS, 3)),
            pltpu.SemaphoreType.DMA((LAYERS, 3)),
            pltpu.SemaphoreType.DMA((2,)),
            pltpu.SemaphoreType.DMA((2,)),
            pltpu.SemaphoreType.DMA((len(NEAR),)),
            pltpu.SemaphoreType.DMA((len(NEAR),)),
        ],
        compiler_params=pltpu.CompilerParams(
            collective_id=0, has_side_effects=True, vmem_limit_bytes=60 * 2**20
        ),
        cost_estimate=pl.CostEstimate(
            flops=17 * 10**9, bytes_accessed=20 * 2**20, transcendentals=0
        ),
        name="trunk",
    )(feat, norm, act, ids, hw, goal, w)


ORDERS = ((1, 2, 4), (2, 1, 4), (4, 1, 2), (4, 2, 1))
CHUNKS = (0, 1, 2, 0, 1, 3)
NEAR = (1, 2, 4)


def flip(index, bit):
    return index + bit - 2 * bit * lax.rem(index // bit, 2)


def scatter_kernel(
    table, term, out,
    mine, send2, keep2, recv2, send3, keep3, recv3, send4, keep4, recv4,
    s1, r1, s2, r2, s3, r3, s4, r4,
    *theirs,
):
    me = lax.axis_index("genome")
    h = lax.axis_index("heads")
    chunks = len(CHUNKS)
    part = mine.shape[-1]
    f32, bf16 = jnp.float32, jnp.bfloat16

    barrier = pltpu.get_barrier_semaphore()
    for bit in NEAR + (8,):
        pl.semaphore_signal(barrier, inc=1, device_id=(flip(me, bit), h), device_id_type=MESH)
    for p in range(chunks):
        for s in range(LIST):
            mine[p, s] = term[s * BLOCK : (s + 1) * BLOCK, p * part : (p + 1) * part]
        mine[p, LIST] = jnp.zeros((BLOCK, part), bf16)
        theirs[p][LIST] = jnp.zeros((BLOCK, part), bf16)
    pl.semaphore_wait(barrier, len(NEAR) + 1)

    def send(src, dst, send_sem, recv_sem, bit):
        cp = pltpu.make_async_remote_copy(
            src, dst, send_sem, recv_sem, device_id=(flip(me, bit), h), device_id_type=MESH
        )
        cp.start()
        return cp

    first, second, third, fourth = {}, {}, {}, {}
    for p in range(chunks):
        first[p] = send(
            mine.at[p, pl.ds(0, LIST)], theirs[p].at[pl.ds(0, LIST)], s1.at[p], r1.at[p],
            ORDERS[CHUNKS[p]][0],
        )

    def stage2(p):
        base = CHUNKS[p] * 32
        first[p].wait()

        def both(j):
            x = mine[p, table[base + j]].astype(f32)
            return x + theirs[p][table[base + 16 + j]].astype(f32)

        @pl.loop(0, 8)
        def _(j):
            send2[p, j] = both(j).astype(bf16)

        second[p] = send(
            send2.at[p], recv2.at[p], s2.at[p], r2.at[p], ORDERS[CHUNKS[p]][1]
        )

        @pl.loop(0, 8)
        def _(j):
            keep2[p, j] = both(8 + j)

    def stage3(p):
        second[p].wait()

        @pl.loop(0, 4)
        def _(j):
            send3[p, j] = (keep2[p, j] + recv2[p, j].astype(f32)).astype(bf16)

        third[p] = send(
            send3.at[p], recv3.at[p], s3.at[p], r3.at[p], ORDERS[CHUNKS[p]][2]
        )

        @pl.loop(0, 4)
        def _(j):
            keep3[p, j] = keep2[p, 4 + j] + recv2[p, 4 + j].astype(f32)

    def stage4(p):
        third[p].wait()
        for j in range(2):
            send4[p, j] = (keep3[p, j] + recv3[p, j].astype(f32)).astype(bf16)
        fourth[p] = send(send4.at[p], recv4.at[p], s4.at[p], r4.at[p], 8)
        for j in range(2):
            keep4[p, j] = keep3[p, 2 + j] + recv3[p, 2 + j].astype(f32)

    def finish(p):
        fourth[p].wait()
        for j in range(2):
            out[j * BLOCK : (j + 1) * BLOCK, p * part : (p + 1) * part] = (
                keep4[p, j] + recv4[p, j].astype(f32)
            )

    for t in range(chunks + 3):
        for lag, stage in enumerate((stage2, stage3, stage4, finish)):
            if 0 <= t - lag < chunks:
                stage(t - lag)


def scatter(table, term):
    c = term.shape[1]
    chunks = len(CHUNKS)
    part = c // chunks
    bf16, f32 = jnp.bfloat16, jnp.float32
    vmem = pl.BlockSpec(memory_space=pltpu.VMEM)

    def buf(count, kind):
        return pltpu.VMEM((chunks, count, BLOCK, part), kind)

    return pl.pallas_call(
        scatter_kernel,
        out_shape=jax.ShapeDtypeStruct((2 * BLOCK, c), f32),
        in_specs=[pl.BlockSpec(memory_space=pltpu.SMEM), vmem],
        out_specs=vmem,
        scratch_shapes=[
            buf(LIST + 1, bf16),
            buf(8, bf16), buf(8, f32), buf(8, bf16),
            buf(4, bf16), buf(4, f32), buf(4, bf16),
            buf(2, bf16), buf(2, f32), buf(2, bf16),
        ]
        + [pltpu.SemaphoreType.DMA((chunks,))] * 8
        + [pltpu.VMEM((LIST + 1, BLOCK, part), bf16)] * chunks,
        compiler_params=pltpu.CompilerParams(
            collective_id=1, has_side_effects=True, vmem_limit_bytes=48 * 2**20
        ),
        name="scatter",
    )(table, term)


def slot_table(lists):
    me = lax.axis_index("genome")
    j = jnp.arange(16, dtype=jnp.int32)
    slot = jnp.arange(LIST, dtype=jnp.int32)
    owners = []
    for one, two, three in ORDERS:
        change = (1 - j // 8) * two + (1 - j // 4 % 2) * three + (1 - j // 2 % 2) * 8
        owners.append((me ^ change) * 2 + j % 2)
    owners = jnp.stack(owners)
    pairs = jnp.stack(
        [jnp.stack([lists[0], lists[1 + NEAR.index(order[0])]]) for order in ORDERS]
    )
    hit = pairs[:, :, None, :] == owners[:, None, :, None]
    return jnp.min(jnp.where(hit, slot, LIST), axis=-1).reshape(-1)


def on_device(
    features_in,
    norm_scale,
    norm_shift,
    conv_weight,
    head_weight,
    assay_head_lists,
    assay_list_counts,
    targets,
):
    ids = assay_head_lists[0]
    norm = jnp.concatenate([norm_scale, norm_shift], axis=0).T
    active = jnp.arange(LIST, dtype=jnp.int32) < assay_list_counts[0]
    act = jnp.repeat(active.astype(jnp.float32), BLOCK)[:, None]
    hw = pick(ids, head_weight)
    goal = targets.reshape(targets.shape[0], LIST * BLOCK)
    own = jnp.pad(assay_head_lists, ((0, 7), (0, BLOCK - LIST)))
    x, term, lists = trunk(features_in, norm, act, own, hw, goal, conv_weight)
    table = slot_table(jnp.concatenate([ids[None], lists[:, 0, :LIST]]))
    return (x, scatter(table, term))


def solution(mesh):
    fits = mesh.shape["genome"] == 16 and mesh.shape["heads"] == 2
    return jax.shard_map(
        on_device if fits else on_device_general,
        mesh=mesh,
        in_specs=(
            P("heads", "genome"),
            P(None, "heads"),
            P(None, "heads"),
            P(None, None, "heads", None),
            P("heads", None),
            P("genome", None),
            P("genome"),
            P("genome", None, None),
        ),
        out_specs=(P("heads", "genome"), P("genome", "heads")),
        check_vma=False,
    )
```

```python
import functools

import jax
import jax.numpy as jnp
from jax import lax
from jax.experimental import pallas as pl
from jax.experimental.pallas import tpu as pltpu
from jax.sharding import PartitionSpec as P

BLOCK = 128
TYPES = 4096
LIST = 4
LAYERS = 2
BASE_DILATION = 4
BIN_DEV = 1024
HEAD_BLOCK_COUNT = 32
HALO = 128
EDGE = 16
MESH = pl.DeviceIdType.MESH


def extended(cells, sides, width):
    for axis, dim in sides:
        count = lax.axis_size(axis)
        ends = count - 1
        head = lax.slice_in_dim(cells, 0, width, axis=dim)
        tail = lax.slice_in_dim(cells, cells.shape[dim] - width, cells.shape[dim], axis=dim)
        cells = jnp.concatenate(
            [
                lax.ppermute(tail, axis, [(i, (i + 1) % count) for i in range(ends)]),
                cells,
                lax.ppermute(head, axis, [((i + 1) % count, i) for i in range(ends)]),
            ],
            axis=dim,
        )
    return cells


def on_device_general(
    features_in,
    norm_scale,
    norm_shift,
    conv_weight,
    head_weight,
    assay_head_lists,
    assay_list_counts,
    targets,
):
    share_cols = features_in.shape[0]
    rows = features_in.shape[1]
    x = features_in
    for layer_index in range(LAYERS):
        dilation_step = BASE_DILATION * 2**layer_index
        taps = conv_weight[layer_index]
        u = jax.nn.gelu(
            x.astype(jnp.float32) * norm_scale[layer_index][:, None]
            + norm_shift[layer_index][:, None],
            approximate=False,
        ).astype(jnp.bfloat16)
        padded_input = extended(u, (("genome", 1),), dilation_step)
        piece = lax.all_gather(padded_input, "heads", axis=0, tiled=True)
        branch = jnp.zeros((share_cols, rows), jnp.float32)
        for k in range(3):
            branch = branch + jnp.dot(
                taps[k],
                piece[:, k * dilation_step : k * dilation_step + rows],
                preferred_element_type=jnp.float32,
            )
        x = (x.astype(jnp.float32) + branch).astype(jnp.bfloat16)
    ids = assay_head_lists[0]
    count = assay_list_counts[0]
    blocks = head_weight.reshape(share_cols, HEAD_BLOCK_COUNT, BLOCK)
    chosen = blocks[:, ids]
    active = (jnp.arange(LIST, dtype=jnp.int32) < count).astype(jnp.float32)
    partial_z = jnp.einsum("ci,cst->ist", x, chosen, preferred_element_type=jnp.float32)
    z = lax.psum(partial_z, "heads")
    slope = (
        (jax.nn.softplus(z) - targets.astype(jnp.float32))
        * jax.nn.sigmoid(z)
        * active[None, :, None]
        / BIN_DEV
    ).astype(jnp.bfloat16)
    term = jnp.einsum("ist,ci->stc", slope, x, preferred_element_type=jnp.float32)
    onehot = (ids[None, :] == jnp.arange(HEAD_BLOCK_COUNT, dtype=jnp.int32)[:, None]).astype(
        jnp.float32
    )
    dense = jnp.einsum("bs,stc->btc", onehot, term).reshape(TYPES, share_cols)
    head_grad = lax.psum_scatter(dense, "genome", scatter_dimension=0, tiled=True)
    return (x, head_grad)


def gelu(v):
    return 0.5 * v * (1.0 + lax.erf(v * 0.7071067811865476))


def pick_kernel(ids_ref, *refs):
    hw_out = refs[LIST]
    for s in range(LIST):
        hw_out[s * BLOCK : (s + 1) * BLOCK, :] = refs[s][...].T


def pick(ids, head_weight):
    c = head_weight.shape[0]
    return pl.pallas_call(
        pick_kernel,
        grid_spec=pltpu.PrefetchScalarGridSpec(
            num_scalar_prefetch=1,
            grid=(1,),
            in_specs=[
                pl.BlockSpec((c, BLOCK), functools.partial(lambda s, i, ids: (0, ids[s]), s))
                for s in range(LIST)
            ],
            out_specs=pl.BlockSpec((LIST * BLOCK, c), lambda i, ids: (0, 0)),
        ),
        out_shape=jax.ShapeDtypeStruct((LIST * BLOCK, c), jnp.bfloat16),
        name="pick",
    )(ids, *[head_weight] * LIST)


def trunk_kernel(
    feat, norm, act, ids, hw, goal, w_hbm,
    x_out, term, lists,
    w, xe, u, acc, edge_out, edge_in, z_own, z_out, z_in,
    tg, w_sem, edge_send, edge_recv, u_send, u_recv, z_send, z_recv, id_send, id_recv,
):
    c, n = feat.shape
    wide = n + HALO
    me = lax.axis_index("genome")
    h = lax.axis_index("heads")
    other = 1 - h
    count = lax.axis_size("genome")
    right, left = lax.rem(me + 1, count), lax.rem(me + count - 1, count)
    dot = functools.partial(jnp.dot, preferred_element_type=jnp.float32)

    loads = []
    for layer in range(LAYERS):
        for side, start in enumerate((h, other)):
            for k in range(3):
                cp = pltpu.make_async_copy(
                    w_hbm.at[layer, k, :, pl.ds(pl.multiple_of(start * c, c), c)],
                    w.at[layer, side, :, pl.ds(k * c, c)],
                    w_sem.at[layer, side, k],
                )
                cp.start()
                loads.append(cp)

    barrier = pltpu.get_barrier_semaphore()
    near = [(flip(me, bit), h) for bit in NEAR]
    for dev in [(me, other), (left, h), (right, h)] + near:
        pl.semaphore_signal(barrier, inc=1, device_id=dev, device_id_type=MESH)

    edge_out[0] = feat[:, 0:BLOCK].astype(jnp.float32).T[:EDGE].astype(jnp.bfloat16)
    edge_out[1] = (
        feat[:, n - BLOCK : n].astype(jnp.float32).T[BLOCK - EDGE :].astype(jnp.bfloat16)
    )
    for s in range(LIST):
        tg[s * BLOCK : (s + 1) * BLOCK, :] = goal[:, s * BLOCK : (s + 1) * BLOCK].T
    pl.semaphore_wait(barrier, 3 + len(near))
    edges = []
    for i, dev in enumerate((left, right)):
        cp = pltpu.make_async_remote_copy(
            edge_out.at[i], edge_in.at[i], edge_send.at[i], edge_recv.at[i],
            device_id=(dev, h), device_id_type=MESH,
        )
        cp.start()
        edges.append(cp)
    asked = []
    for i, dev in enumerate(near):
        cp = pltpu.make_async_remote_copy(
            ids, lists.at[i], id_send.at[i], id_recv.at[i],
            device_id=dev, device_id_type=MESH,
        )
        cp.start()
        asked.append(cp)

    lane = lax.broadcasted_iota(jnp.int32, (1, wide), 1)
    inside = jnp.where(
        lane < n,
        1.0,
        jnp.where(
            lane < n + HALO // 2,
            jnp.where(me < count - 1, 1.0, 0.0),
            jnp.where(me > 0, 1.0, 0.0),
        ),
    ).astype(jnp.float32)

    pieces = 3
    step = c // pieces

    tiles = [(0, n // 2), (n // 2, n // 2), (n, HALO)]

    def u_copy(layer, m):
        if layer == 0:
            part = (pl.ds(c + m * step, step), slice(None))
        else:
            part = (pl.ds(c, c), pl.ds(*tiles[m]))
        return pltpu.make_async_remote_copy(
            u.at[(layer, 0) + part], u.at[(layer, 1) + part],
            u_send.at[layer, m], u_recv.at[layer, m],
            device_id=(me, other), device_id_type=MESH,
        )

    def shift(layer, side):
        d = BASE_DILATION * 2**layer

        @pl.loop(0, c // BLOCK)
        def _(j):
            def rows(k):
                return pl.ds(pl.multiple_of(k * c + j * BLOCK, BLOCK), BLOCK)

            val = u[layer, side, rows(1), :].astype(jnp.float32)
            u[layer, side, rows(0), :] = pltpu.roll(val, d, 1).astype(jnp.bfloat16)
            u[layer, side, rows(2), :] = pltpu.roll(val, wide - d, 1).astype(jnp.bfloat16)

    def active(layer, rows, v, mask):
        a = norm[rows, layer : layer + 1]
        b = norm[rows, LAYERS + layer : LAYERS + layer + 1]
        val = gelu(v.astype(jnp.float32) * a + b)
        return (val if mask is None else val * mask).astype(jnp.bfloat16)

    def activate(layer, lanes):
        start, size = lanes

        @pl.loop(0, c // BLOCK)
        def _(j):
            rows = pl.ds(pl.multiple_of(j * BLOCK, BLOCK), BLOCK)
            u[layer, 0, pl.ds(pl.multiple_of(c + j * BLOCK, BLOCK), BLOCK), pl.ds(start, size)] = (
                active(
                    layer,
                    rows,
                    xe[layer, rows, pl.ds(start, size)],
                    inside[:, start:] if start == n else None,
                )
            )

    @pl.loop(0, c // BLOCK)
    def _(j):
        rows = pl.ds(pl.multiple_of(j * BLOCK, BLOCK), BLOCK)
        val = feat[rows, :]
        xe[0, rows, 0:n] = val
        u[0, 0, pl.ds(pl.multiple_of(c + j * BLOCK, BLOCK), BLOCK), 0:n] = active(
            0, rows, val, None
        )

    for cp in edges:
        cp.wait()
    halo = jnp.concatenate(
        [
            edge_in[0].astype(jnp.float32),
            jnp.zeros((HALO - 2 * EDGE, c), jnp.float32),
            edge_in[1].astype(jnp.float32),
        ],
        axis=0,
    )
    halo = halo.T
    xe[0, :, n:wide] = halo.astype(jnp.bfloat16)
    u[0, 0, c : 2 * c, n:wide] = active(0, slice(None), halo, inside[:, n:wide])

    copies = []
    for m in range(pieces):
        cp = u_copy(0, m)
        cp.start()
        copies.append(cp)

    for layer in range(LAYERS):
        last = layer == LAYERS - 1
        here = tiles[:2] if last else tiles
        shift(layer, 0)
        for k in range(3):
            loads[6 * layer + k].wait()
        for start, size in here:
            acc[:, start : start + size] = dot(
                w[layer, 0], u[layer, 0, :, start : start + size]
            )
        for cp in copies:
            cp.wait()
        shift(layer, 1)
        for k in range(3):
            loads[6 * layer + 3 + k].wait()
        copies = []
        for m, (start, size) in enumerate(here):
            lanes = slice(start, start + size)
            t = acc[:, lanes] + dot(w[layer, 1], u[layer, 1, :, lanes])
            val = (xe[layer, :, lanes].astype(jnp.float32) + t).astype(jnp.bfloat16)
            if last:
                x_out[:, lanes] = val
            else:
                xe[layer + 1, :, lanes] = val
                activate(layer + 1, tiles[m])
                cp = u_copy(layer + 1, m)
                cp.start()
                copies.append(cp)

    groups = 2
    size = LIST * BLOCK // groups
    sums = []
    for s in range(groups):
        rows = pl.ds(s * size, size)
        part = dot(hw[rows, :], x_out[...])
        z_own[rows, :] = part
        z_out[rows, :] = part.astype(jnp.bfloat16)
        cp = pltpu.make_async_remote_copy(
            z_out.at[rows], z_in.at[rows], z_send.at[s], z_recv.at[s],
            device_id=(me, other), device_id_type=MESH,
        )
        cp.start()
        sums.append(cp)
    for s in range(groups):
        rows = pl.ds(s * size, size)
        sums[s].wait()
        z = z_own[rows, :] + z_in[rows, :].astype(jnp.float32)
        e = jnp.exp(-jnp.abs(z))
        soft = jnp.maximum(z, 0.0) + jnp.log1p(e)
        sig = jnp.where(z >= 0.0, 1.0, e) / (1.0 + e)
        slope = (
            (soft - tg[rows, :].astype(jnp.float32)) * sig * (act[rows, :] / BIN_DEV)
        ).astype(jnp.bfloat16)
        term[rows, :] = lax.dot_general(
            slope, x_out[...], (((1,), (1,)), ((), ())), preferred_element_type=jnp.float32
        ).astype(jnp.bfloat16)
    for cp in asked:
        cp.wait()


def trunk(feat, norm, act, ids, hw, goal, w):
    c, n = feat.shape
    wide = n + HALO
    vmem = pl.BlockSpec(memory_space=pltpu.VMEM)
    bf16, f32 = jnp.bfloat16, jnp.float32
    return pl.pallas_call(
        trunk_kernel,
        out_shape=[
            jax.ShapeDtypeStruct((c, n), bf16),
            jax.ShapeDtypeStruct((LIST * BLOCK, c), bf16),
            jax.ShapeDtypeStruct((len(NEAR),) + ids.shape, jnp.int32),
        ],
        in_specs=[vmem] * 6 + [pl.BlockSpec(memory_space=pl.ANY)],
        out_specs=[vmem, vmem, vmem],
        scratch_shapes=[
            pltpu.VMEM((LAYERS, 2, c, 3 * c), bf16),
            pltpu.VMEM((LAYERS, c, wide), bf16),
            pltpu.VMEM((LAYERS, 2, 3 * c, wide), bf16),
            pltpu.VMEM((c, wide), f32),
            pltpu.VMEM((2, EDGE, c), bf16),
            pltpu.VMEM((2, EDGE, c), bf16),
            pltpu.VMEM((LIST * BLOCK, n), f32),
            pltpu.VMEM((LIST * BLOCK, n), bf16),
            pltpu.VMEM((LIST * BLOCK, n), bf16),
            pltpu.VMEM((LIST * BLOCK, n), bf16),
            pltpu.SemaphoreType.DMA((LAYERS, 2, 3)),
            pltpu.SemaphoreType.DMA((2,)),
            pltpu.SemaphoreType.DMA((2,)),
            pltpu.SemaphoreType.DMA((LAYERS, 3)),
            pltpu.SemaphoreType.DMA((LAYERS, 3)),
            pltpu.SemaphoreType.DMA((2,)),
            pltpu.SemaphoreType.DMA((2,)),
            pltpu.SemaphoreType.DMA((len(NEAR),)),
            pltpu.SemaphoreType.DMA((len(NEAR),)),
        ],
        compiler_params=pltpu.CompilerParams(
            collective_id=0, has_side_effects=True, vmem_limit_bytes=60 * 2**20
        ),
        cost_estimate=pl.CostEstimate(
            flops=17 * 10**9, bytes_accessed=20 * 2**20, transcendentals=0
        ),
        name="trunk",
    )(feat, norm, act, ids, hw, goal, w)


ORDERS = ((1, 2, 4), (2, 1, 4), (4, 1, 2), (4, 2, 1))
CHUNKS = (0, 1, 2, 0, 1, 3)
NEAR = (1, 2, 4)


def flip(index, bit):
    return index + bit - 2 * bit * lax.rem(index // bit, 2)


def scatter_kernel(
    table, term, out,
    mine, send2, keep2, recv2, send3, keep3, recv3, send4, keep4, recv4,
    s1, r1, s2, r2, s3, r3, s4, r4,
    *theirs,
):
    me = lax.axis_index("genome")
    h = lax.axis_index("heads")
    chunks = len(CHUNKS)
    part = mine.shape[-1]
    f32, bf16 = jnp.float32, jnp.bfloat16

    barrier = pltpu.get_barrier_semaphore()
    for bit in NEAR + (8,):
        pl.semaphore_signal(barrier, inc=1, device_id=(flip(me, bit), h), device_id_type=MESH)
    for p in range(chunks):
        for s in range(LIST):
            mine[p, s] = term[s * BLOCK : (s + 1) * BLOCK, p * part : (p + 1) * part]
        mine[p, LIST] = jnp.zeros((BLOCK, part), bf16)
        theirs[p][LIST] = jnp.zeros((BLOCK, part), bf16)
    pl.semaphore_wait(barrier, len(NEAR) + 1)

    def send(src, dst, send_sem, recv_sem, bit):
        cp = pltpu.make_async_remote_copy(
            src, dst, send_sem, recv_sem, device_id=(flip(me, bit), h), device_id_type=MESH
        )
        cp.start()
        return cp

    first, second, third, fourth = {}, {}, {}, {}
    for p in range(chunks):
        first[p] = send(
            mine.at[p, pl.ds(0, LIST)], theirs[p].at[pl.ds(0, LIST)], s1.at[p], r1.at[p],
            ORDERS[CHUNKS[p]][0],
        )

    def stage2(p):
        base = CHUNKS[p] * 32
        first[p].wait()

        def both(j):
            x = mine[p, table[base + j]].astype(f32)
            return x + theirs[p][table[base + 16 + j]].astype(f32)

        @pl.loop(0, 8)
        def _(j):
            send2[p, j] = both(j).astype(bf16)

        second[p] = send(
            send2.at[p], recv2.at[p], s2.at[p], r2.at[p], ORDERS[CHUNKS[p]][1]
        )

        @pl.loop(0, 8)
        def _(j):
            keep2[p, j] = both(8 + j)

    def stage3(p):
        second[p].wait()

        @pl.loop(0, 4)
        def _(j):
            send3[p, j] = (keep2[p, j] + recv2[p, j].astype(f32)).astype(bf16)

        third[p] = send(
            send3.at[p], recv3.at[p], s3.at[p], r3.at[p], ORDERS[CHUNKS[p]][2]
        )

        @pl.loop(0, 4)
        def _(j):
            keep3[p, j] = keep2[p, 4 + j] + recv2[p, 4 + j].astype(f32)

    def stage4(p):
        third[p].wait()
        for j in range(2):
            send4[p, j] = (keep3[p, j] + recv3[p, j].astype(f32)).astype(bf16)
        fourth[p] = send(send4.at[p], recv4.at[p], s4.at[p], r4.at[p], 8)
        for j in range(2):
            keep4[p, j] = keep3[p, 2 + j] + recv3[p, 2 + j].astype(f32)

    def finish(p):
        fourth[p].wait()
        for j in range(2):
            out[j * BLOCK : (j + 1) * BLOCK, p * part : (p + 1) * part] = (
                keep4[p, j] + recv4[p, j].astype(f32)
            )

    for t in range(chunks + 3):
        for lag, stage in enumerate((stage2, stage3, stage4, finish)):
            if 0 <= t - lag < chunks:
                stage(t - lag)


def scatter(table, term):
    c = term.shape[1]
    chunks = len(CHUNKS)
    part = c // chunks
    bf16, f32 = jnp.bfloat16, jnp.float32
    vmem = pl.BlockSpec(memory_space=pltpu.VMEM)

    def buf(count, kind):
        return pltpu.VMEM((chunks, count, BLOCK, part), kind)

    return pl.pallas_call(
        scatter_kernel,
        out_shape=jax.ShapeDtypeStruct((2 * BLOCK, c), f32),
        in_specs=[pl.BlockSpec(memory_space=pltpu.SMEM), vmem],
        out_specs=vmem,
        scratch_shapes=[
            buf(LIST + 1, bf16),
            buf(8, bf16), buf(8, f32), buf(8, bf16),
            buf(4, bf16), buf(4, f32), buf(4, bf16),
            buf(2, bf16), buf(2, f32), buf(2, bf16),
        ]
        + [pltpu.SemaphoreType.DMA((chunks,))] * 8
        + [pltpu.VMEM((LIST + 1, BLOCK, part), bf16)] * chunks,
        compiler_params=pltpu.CompilerParams(
            collective_id=1, has_side_effects=True, vmem_limit_bytes=48 * 2**20
        ),
        name="scatter",
    )(table, term)


def slot_table(lists):
    me = lax.axis_index("genome")
    j = jnp.arange(16, dtype=jnp.int32)
    slot = jnp.arange(LIST, dtype=jnp.int32)
    owners = []
    for one, two, three in ORDERS:
        change = (1 - j // 8) * two + (1 - j // 4 % 2) * three + (1 - j // 2 % 2) * 8
        owners.append((me ^ change) * 2 + j % 2)
    owners = jnp.stack(owners)
    pairs = jnp.stack(
        [jnp.stack([lists[0], lists[1 + NEAR.index(order[0])]]) for order in ORDERS]
    )
    hit = pairs[:, :, None, :] == owners[:, None, :, None]
    return jnp.min(jnp.where(hit, slot, LIST), axis=-1).reshape(-1)


def on_device(
    features_in,
    norm_scale,
    norm_shift,
    conv_weight,
    head_weight,
    assay_head_lists,
    assay_list_counts,
    targets,
):
    ids = assay_head_lists[0]
    norm = jnp.concatenate([norm_scale, norm_shift], axis=0).T
    active = jnp.arange(LIST, dtype=jnp.int32) < assay_list_counts[0]
    act = jnp.repeat(active.astype(jnp.float32), BLOCK)[:, None]
    hw = pick(ids, head_weight)
    goal = targets.reshape(targets.shape[0], LIST * BLOCK)
    own = jnp.pad(assay_head_lists, ((0, 7), (0, BLOCK - LIST)))
    x, term, lists = trunk(features_in, norm, act, own, hw, goal, conv_weight)
    table = slot_table(jnp.concatenate([ids[None], lists[:, 0, :LIST]]))
    return (x, scatter(table, term))


def solution(mesh):
    fits = mesh.shape["genome"] == 16 and mesh.shape["heads"] == 2
    return jax.shard_map(
        on_device if fits else on_device_general,
        mesh=mesh,
        in_specs=(
            P("heads", "genome"),
            P(None, "heads"),
            P(None, "heads"),
            P(None, None, "heads", None),
            P("heads", None),
            P("genome", None),
            P("genome"),
            P("genome", None, None),
        ),
        out_specs=(P("heads", "genome"), P("genome", "heads")),
        check_vma=False,
    )
```
